32 devices in a mesh: tm: 4 (over y, x), tok: 8 (over z, core).
Axes of the slice: x: 2, y: 2, z: 4, core: 2. Of those that a mesh axis runs over, the one named last changes fastest.
Arguments:
- start: bfloat16 [1024, 1536], P('tok'), may hold values from -6 to 6
- trajectory: bfloat16 [8, 1024, 1536], P('tm', 'tok'), may hold values from -6 to 6
- plan: int32 [9], replicated, may hold values from 0 to 1000, as said below
- neighbors: int32 [16, 3], P('tok'), may hold values from 0 to 15, as said below
- mod_weight: bfloat16 [256, 3072], replicated, may hold values from -0.75 to 0.75
- w_qkv: bfloat16 [1536, 4608], P('tok'), may hold values from -0.15625 to 0.15625
- w_out: bfloat16 [1536, 1536], P('tok'), may hold values from -1.25 to 1.25
Outputs:
- updated: float32 [8, 1024, 1536], P('tm', 'tok')
The draws below stay inside these ranges and needn't reach their ends.
Inputs may be any that keep to these rules, and one draw needn't show every extreme that they name: `plan`: strictly decreasing from 1000 at the first entry to 0 at the last. `neighbors`: entry 0 of row c is c; the other entries lie within 2 of c.
All inputs are finite; a program needn't handle non-finite values.
Results may differ from the reference program's by a relative error of at most 0.0045.
Values may be sent and summed in bfloat16 or wider, within the bound.
No kernel may reach another device: no remote copies, remote signals or barrier semaphores. Data moves between devices by JAX's collectives and lax.ppermute only.
A program may use at most 128 MiB of HBM per device.

```python
import math
import jax
import jax.numpy as jnp
from jax import lax

HEADS = 12
HEAD_DIM = 128
TEMB = 256
NSCHED = 1000
NB = 3
D = 1536
TILE = 64
TSTEPS = 8
TOKENS = 1024
NTILES = 16


def draw_plan(key, part):
    inner = jax.random.permutation(key, NSCHED - 1)[:TSTEPS - 1] + 1
    inner = -jnp.sort(-inner)
    head = jnp.full((1,), NSCHED, jnp.int32)
    tail = jnp.zeros((1,), jnp.int32)
    return jnp.concatenate([head, inner.astype(jnp.int32), tail]).astype(jnp.int32)


def draw_neighbors(key, part):
    offsets = jnp.array([-2, -1, 1, 2], jnp.int32)
    keys = jax.random.split(key, NTILES)
    picks = jax.vmap(lambda one: jax.random.permutation(one, 4))(keys)[:, :2]
    chosen = offsets[picks]
    own = jnp.arange(NTILES, dtype=jnp.int32)[:, None]
    target = own + chosen
    outside = (target < 0) | (target >= NTILES)
    target = jnp.where(outside, own - chosen, target)
    return jnp.concatenate([own, target], axis=1).astype(jnp.int32)


def block_scale(rng, shape, cuts, least, top_value):
    def one(position, shards_of):
        steps = jax.random.uniform(jax.random.fold_in(jax.random.fold_in(rng, 6), position), (shards_of,), jnp.float32, least / len(cuts), top_value / len(cuts))
        return jnp.repeat(jnp.exp(steps), shape[position] // shards_of).reshape((-1,) + (1,) * (len(shape) - position - 1))

    level = one(*cuts[0])
    for cut in cuts[1:]:
        level = level * one(*cut)
    return level


def centred(stream_key, extent, scale, most, cuts=(), kind=jnp.bfloat16):
    result = scale * jax.random.normal(stream_key, extent, jnp.float32)
    if cuts:
        result = result * block_scale(stream_key, extent, cuts, -0.22, 0.18)
    return jnp.clip(result, -most, most).astype(kind)


def setup_inputs(seed: int = 0) -> dict:
    key_of = jax.random.split(jax.random.key(seed), 8)
    start = centred(key_of[0], (TOKENS, D), 1.0, 6.0, ((0, 8),))
    trajectory = centred(key_of[1], (TSTEPS, TOKENS, D), 1.0, 6.0, ((0, 4), (1, 8)))
    plan = draw_plan(jax.random.fold_in(key_of[7], 71), 0)
    neighbors = draw_neighbors(jax.random.fold_in(key_of[7], 71), 0)
    mod_weight = centred(key_of[4], (TEMB, 2 * D), (TEMB // 4) ** -0.5, 0.75)
    w_qkv = centred(key_of[5], (D, 3 * D), D ** -0.5, 0.15625, ((0, 8),))
    w_out = centred(key_of[6], (D, D), (D // 64) ** -0.5, 1.25, ((0, 8),))
    return {"start": start, "trajectory": trajectory, "plan": plan, "neighbors": neighbors, "mod_weight": mod_weight, "w_qkv": w_qkv, "w_out": w_out}


def time_mod(times, mod_weight):
    half = TEMB // 2
    freqs = jnp.exp(-math.log(10000.0) * jnp.arange(half, dtype=jnp.float32) / half)
    angle = 1000.0 * times[:, None] * freqs[None, :]
    embed = jnp.concatenate([jnp.cos(angle), jnp.sin(angle)], axis=1)
    act = jax.nn.silu(embed).astype(jnp.bfloat16)
    return jnp.dot(act, mod_weight, preferred_element_type=jnp.float32)

def modulate(state, shift, scale):
    values = state.astype(jnp.float32)
    center = values - lax.optimization_barrier(jnp.mean(values, -1, keepdims=True))
    spread = lax.optimization_barrier(jnp.mean(center * center, -1, keepdims=True))
    return (center / jnp.sqrt(spread + 1e-06) * (1.0 + scale) + shift).astype(jnp.bfloat16)

def head_norm(values):
    return (values / jnp.sqrt(lax.optimization_barrier(jnp.mean(values * values, -1, keepdims=True)) + 1e-06)).astype(jnp.bfloat16)

def drift_one(state, shift, scale, neighbors, w_qkv, w_out):
    normed = modulate(state, shift[None, :], scale[None, :])
    qkv = jnp.dot(normed, w_qkv, preferred_element_type=jnp.float32)
    query = head_norm(qkv[:, :D].reshape(NTILES, TILE, HEADS, HEAD_DIM))
    keys = head_norm(qkv[:, D:2 * D].reshape(NTILES, TILE, HEADS, HEAD_DIM))
    values = qkv[:, 2 * D:].astype(jnp.bfloat16).reshape(NTILES, TILE, HEADS, HEAD_DIM)
    near_keys = jnp.take(keys, neighbors, axis=0).reshape(NTILES, NB * TILE, HEADS, HEAD_DIM)
    near_values = jnp.take(values, neighbors, axis=0).reshape(NTILES, NB * TILE, HEADS, HEAD_DIM)
    score = jnp.einsum('cqha,ckha->chqk', query.astype(jnp.float32), near_keys.astype(jnp.float32)) / math.sqrt(HEAD_DIM)
    expo = jnp.exp(score)
    prob = (expo / lax.optimization_barrier(jnp.sum(expo, -1, keepdims=True))).astype(jnp.bfloat16)
    attn = jnp.einsum('chqk,ckha->cqha', prob.astype(jnp.float32), near_values.astype(jnp.float32))
    attn = attn.astype(jnp.bfloat16).reshape(TOKENS, D)
    return jnp.dot(attn, w_out, preferred_element_type=jnp.float32)

def reference(start, trajectory, plan, neighbors, mod_weight, w_qkv, w_out):
    times = plan.astype(jnp.float32) / NSCHED
    steps = times[:-1] - times[1:]
    mod = time_mod(times[:TSTEPS], mod_weight)

    def single(item):
        state, shift, scale = item
        return drift_one(state, shift, scale, neighbors, w_qkv, w_out)
    drift = lax.map(single, (trajectory, mod[:, :D], mod[:, D:]))
    scaled = steps[:, None, None] * drift
    before = jnp.cumsum(scaled, axis=0) - scaled
    return start.astype(jnp.float32)[None] - before
```

```python
import functools
import math

import jax
import jax.numpy as jnp
from jax import lax
from jax.experimental import pallas as pl
from jax.experimental.pallas import tpu as pltpu
from jax.sharding import PartitionSpec as P

HEADS = 12
HEAD_DIM = 128
NSCHED = 1000
CORES = 2
VMEM_LIMIT = 48 * 1024 * 1024
ANY = pl.BlockSpec(memory_space=pl.ANY)
VMEM = pl.BlockSpec(memory_space=pltpu.VMEM)
SMEM = pl.BlockSpec(memory_space=pltpu.SMEM)


def call(kernel, outs, in_specs, out_specs, scratch, flops, nbytes):
    return pl.pallas_call(
        kernel,
        out_shape=outs,
        in_specs=in_specs,
        out_specs=out_specs,
        scratch_shapes=scratch,
        compiler_params=pltpu.CompilerParams(vmem_limit_bytes=VMEM_LIMIT),
        cost_estimate=pl.CostEstimate(flops=flops, bytes_accessed=nbytes, transcendentals=0),
    )


def head_groups(size):
    groups = 1
    while size % (2 * groups) == 0 and HEADS % (2 * groups) == 0:
        groups *= 2
    return groups


def swap(value, axis, mask):
    return lax.ppermute(value, axis, [(i, i ^ mask) for i in range(lax.axis_size(axis))])


def cut_kernel(group_cols, g_ref, wqkv, wout, first, second, sems):
    width = wout.shape[1]
    at = pl.multiple_of(g_ref[0] * group_cols, group_cols)
    sources = (
        (wqkv, width, first, 0),
        (wqkv, 2 * width, first, 1),
        (wqkv, 0, second, 0),
        (wout, 0, second, 1),
    )
    copies = [
        pltpu.make_async_copy(
            src.at[:, pl.ds(pl.multiple_of(base + at, group_cols), group_cols)],
            dst.at[:, pl.ds(slot * group_cols, group_cols)],
            sems.at[n],
        )
        for n, (src, base, dst, slot) in enumerate(sources)
    ]
    for copy in copies:
        copy.start()
    for copy in copies:
        copy.wait()


def modulate_kernel(act, weight, state, *outs):
    mod = jnp.dot(act[...], weight[...], preferred_element_type=jnp.float32)
    width = state.shape[-1]
    for i, out in enumerate(outs):
        values = state[i].astype(jnp.float32)
        center = values - jnp.mean(values, -1, keepdims=True)
        spread = jnp.mean(center * center, -1, keepdims=True)
        shift = mod[i : i + 1, :width]
        scale = mod[i : i + 1, width:]
        out[...] = (center / jnp.sqrt(spread + 1e-06) * (1.0 + scale) + shift).astype(jnp.bfloat16)


def head_norm(values):
    return values / jnp.sqrt(jnp.mean(values * values, -1, keepdims=True) + 1e-06)


def load_all(copies, sems):
    made = [pltpu.make_async_copy(src, dst, sems.at[n]) for n, (src, dst) in enumerate(copies)]
    for copy in made:
        copy.start()
    for copy in made:
        copy.wait()


def project_kernel(plan, where, *refs):
    states, pieces = refs[: plan["states"]], refs[plan["states"] : plan["states"] + plan["pieces"]]
    out, held, weight, sems = refs[plan["states"] + plan["pieces"] :]
    tokens, steps_here, kept, columns = plan["tokens"], plan["steps"], plan["kept"], plan["columns"]
    depth = pieces[0].shape[0]
    copies = []
    for n, state in enumerate(states):
        slot, i = divmod(n, steps_here)
        time = (where[0] ^ slot) * steps_here + i
        copies.append((state, held.at[pl.ds(pl.multiple_of(time * tokens, tokens), tokens), :]))
    for n, piece in enumerate(pieces):
        row = where[1 + n]
        copies.append(
            (
                piece.at[:, pl.ds(columns[0], columns[1])],
                weight.at[pl.ds(pl.multiple_of(row * depth, depth), depth), :],
            )
        )
    load_all(copies, sems)
    at = 0
    while at < kept:
        count = min(2, kept - at)
        rows = slice(at * tokens, (at + count) * tokens)
        product = jnp.dot(held[rows, :], weight[...], preferred_element_type=jnp.float32)
        for head in range(columns[1] // HEAD_DIM):
            cols = slice(head * HEAD_DIM, (head + 1) * HEAD_DIM)
            values = product[:, cols]
            if head < plan["normed"]:
                values = head_norm(values)
            out[at : at + count, :, cols] = values.astype(jnp.bfloat16).reshape(count, tokens, HEAD_DIM)
        at += count


def attention_kernel(groups, steps_here, prefixes, g_ref, steps, mask, query, own, low, high, *refs):
    outs, total, before = refs[:groups], refs[groups], refs[groups + 1]
    kept, tokens, columns = query.shape
    heads = columns // HEAD_DIM
    weights = mask[...]
    total[...] = jnp.zeros_like(total)
    before[0] = jnp.zeros(before.shape[1:], jnp.bfloat16)
    for k in range(kept):
        for head in range(heads):
            cols = slice(head * HEAD_DIM, (head + 1) * HEAD_DIM)
            vcols = slice(columns + head * HEAD_DIM, columns + (head + 1) * HEAD_DIM)
            keys = jnp.concatenate([low[k, :, cols], own[k, :, cols], high[k, :, cols]], axis=0)
            values = jnp.concatenate([low[k, :, vcols], own[k, :, vcols], high[k, :, vcols]], axis=0)
            score = lax.dot_general(
                query[k, :, cols],
                keys,
                (((1,), (1,)), ((), ())),
                preferred_element_type=jnp.float32,
            ) * (1.0 / math.sqrt(HEAD_DIM))
            expo = jnp.exp(score) * weights
            prob = (expo / jnp.sum(expo, -1, keepdims=True)).astype(jnp.bfloat16)
            attn = jnp.dot(prob, values, preferred_element_type=jnp.float32)
            total[:, cols] += steps[k] * attn.astype(jnp.bfloat16).astype(jnp.float32)
        before[k + 1] = total[...].astype(jnp.bfloat16)
    for slot, out in enumerate(outs):
        first = (g_ref[0] ^ slot) * steps_here
        for i in range(steps_here):
            out[i] = before[first + i]


def out_kernel(groups, parts, where, start, *refs):
    sums = refs[:groups]
    pieces = refs[groups : groups + groups * len(parts)]
    out, weight, sems = refs[groups + groups * len(parts) :]
    steps_here, tokens, columns = sums[0].shape
    copies = []
    for slot in range(groups):
        for n, blocks in enumerate(parts):
            piece = pieces[slot * len(parts) + n]
            depth = piece.shape[0] // len(blocks)
            for b, place in enumerate(blocks):
                row = where[1 + place]
                copies.append(
                    (
                        piece.at[pl.ds(b * depth, depth), :],
                        weight.at[slot, pl.ds(pl.multiple_of(row * depth, depth), depth), :],
                    )
                )
    load_all(copies, sems)
    left = [value[...].reshape(steps_here * tokens, columns) for value in sums]
    for slot in range(groups):
        drift = jnp.zeros((steps_here * tokens, columns), jnp.float32)
        for other in range(groups):
            rows = pl.ds(pl.multiple_of((where[0] ^ other) * columns, columns), columns)
            drift += jnp.dot(left[other], weight[slot, rows, :], preferred_element_type=jnp.float32)
        cols = pl.ds(pl.multiple_of((where[0] ^ slot) * columns, columns), columns)
        base = start[:, cols].astype(jnp.float32)
        for i in range(steps_here):
            out[i, :, cols] = base - drift[i * tokens : (i + 1) * tokens]


def gather_rows(piece):
    chips = lax.axis_size("tok") // CORES
    across = swap(piece, "tok", 2 * CORES)
    beside = swap(piece, "tok", CORES)
    middle = lax.ppermute(
        piece, "tok", [(c * CORES + p, (c ^ 3) * CORES + p) for c in (1, 2) for p in range(CORES)]
    )
    relay = lax.ppermute(
        across, "tok", [(c * CORES + p, (c ^ 1) * CORES + p) for c in (1, 2) for p in range(CORES)]
    )
    chip = lax.axis_index("tok") // CORES
    inner = (chip > 0) & (chip < chips - 1)
    return [piece, across, beside, jnp.where(inner, middle, relay)]


def body(start, trajectory, plan, neighbors, mod_weight, w_qkv, w_out):
    steps_here, tokens, width = trajectory.shape
    tm, tok = lax.axis_size("tm"), lax.axis_size("tok")
    groups = head_groups(tm)
    spans = tm // groups
    columns = width // groups
    depth = w_qkv.shape[0]
    index, place = lax.axis_index("tm"), lax.axis_index("tok")
    group, span = index % groups, index // groups
    chip, core = place // CORES, place % CORES
    count = groups * steps_here
    kept = count - 1 if spans == 1 else count
    bf16 = jnp.bfloat16
    g = group.astype(jnp.int32).reshape(1)

    first, second = call(
        functools.partial(cut_kernel, columns),
        [jax.ShapeDtypeStruct((depth, 2 * columns), bf16)] * 2,
        [SMEM, ANY, ANY],
        [ANY, ANY],
        [pltpu.SemaphoreType.DMA((4,))],
        0,
        4 * depth * columns * 4,
    )(g, w_qkv, w_out)

    times = plan.astype(jnp.float32) / NSCHED
    own_times = lax.dynamic_slice_in_dim(times, index * steps_here, steps_here)
    span_times = lax.dynamic_slice_in_dim(times, span * count, count + 1)
    steps = span_times[:-1] - span_times[1:]
    half = mod_weight.shape[0] // 2
    freqs = jnp.exp(-math.log(10000.0) * jnp.arange(half, dtype=jnp.float32) / half)
    angle = 1000.0 * own_times[:, None] * freqs[None, :]
    embed = jnp.concatenate([jnp.cos(angle), jnp.sin(angle)], axis=1)
    act = jnp.pad(jax.nn.silu(embed).astype(bf16), ((0, -steps_here % 16), (0, 0)))
    normed = call(
        modulate_kernel,
        [jax.ShapeDtypeStruct((tokens, width), bf16)] * steps_here,
        [VMEM] * 3,
        [VMEM] * steps_here,
        [],
        2 * 16 * mod_weight.size,
        2 * mod_weight.size + 4 * trajectory.size,
    )(act, mod_weight, trajectory)

    states = [list(normed)]
    if groups == 4 and steps_here > 1:
        cut = steps_here // 2
        beside = [swap(v, "tm", 1) for v in normed]
        across = [swap(v, "tm", 2) for v in normed]
        far = [swap(v, "tm", 2) for v in beside[:cut]] + [swap(v, "tm", 1) for v in across[cut:]]
        states += [beside, across, far]
    else:
        states += [[swap(v, "tm", s) for v in normed] for s in range(1, groups)]
    flat_states = [v for slot in states for v in slot]

    if tok == 4 * CORES:
        masks = (0, 2, 1, 3)
        first_mine = gather_rows(first)
        first_pieces = first_mine + [swap(v, "tok", 1) for v in first_mine]
        second_mine = gather_rows(second)
        second_pieces = second_mine + [swap(v, "tok", 1) for v in second_mine]
        rows = jnp.stack(
            [(chip ^ m) * CORES + core for m in masks] + [(chip ^ m) * CORES + 1 - core for m in masks]
        )
        half_out = jnp.concatenate([v[:, columns:] for v in second_mine], axis=0)
        mine = [half_out] + [swap(half_out, "tm", s) for s in range(1, groups)]
        out_pieces = [[v, swap(v, "tok", 1)] for v in mine]
        parts = ((0, 1, 2, 3), (4, 5, 6, 7))
    else:
        first_pieces = [lax.all_gather(first, "tok", axis=0, tiled=True)]
        second_pieces = [lax.all_gather(second, "tok", axis=0, tiled=True)]
        rows = jnp.zeros((1,), jnp.int32)
        whole = second_pieces[0][:, columns:]
        out_pieces = [[whole]] + [[swap(whole, "tm", s)] for s in range(1, groups)]
        parts = ((0,),)
    where = jnp.concatenate([g, rows.astype(jnp.int32)])

    def project(pieces, cols, normed_heads):
        info = {
            "states": len(flat_states),
            "pieces": len(pieces),
            "tokens": tokens,
            "steps": steps_here,
            "kept": kept,
            "columns": cols,
            "normed": normed_heads,
        }
        return call(
            functools.partial(project_kernel, info),
            jax.ShapeDtypeStruct((kept, tokens, cols[1]), bf16),
            [SMEM] + [ANY] * (len(flat_states) + len(pieces)),
            VMEM,
            [
                pltpu.VMEM((count * tokens, width), bf16),
                pltpu.VMEM((width, cols[1]), bf16),
                pltpu.SemaphoreType.DMA((len(flat_states) + len(pieces),)),
            ],
            2 * kept * tokens * width * cols[1],
            2 * (kept * tokens * (width + cols[1]) + width * cols[1]),
        )(where, *flat_states, *pieces)

    heads = columns // HEAD_DIM
    kv = project(first_pieces, (0, 2 * columns), heads)
    low = lax.ppermute(kv, "tok", [(i, i + 1) for i in range(tok - 1)])
    high = lax.ppermute(kv, "tok", [(i + 1, i) for i in range(tok - 1)])
    query = project(second_pieces, (0, columns), heads)

    tile = tokens // 2
    local = neighbors - (2 * place - 2)
    times_listed = jnp.sum(
        (local[:, :, None] == jnp.arange(6, dtype=jnp.int32)[None, None, :]).astype(jnp.float32), axis=1
    )
    mask = jnp.repeat(jnp.repeat(times_listed, tile, axis=0), tile, axis=1)
    summed = jax.ShapeDtypeStruct((steps_here, tokens, columns), bf16)
    sums = call(
        functools.partial(attention_kernel, groups, steps_here, kept + 1),
        [summed] * groups + ([] if spans == 1 else [jax.ShapeDtypeStruct((tokens, columns), jnp.float32)]),
        [SMEM, SMEM] + [VMEM] * 5,
        [VMEM] * (groups if spans == 1 else groups + 1),
        ([pltpu.VMEM((tokens, columns), jnp.float32)] if spans == 1 else [])
        + [pltpu.VMEM((kept + 1, tokens, columns), bf16)],
        8 * kept * tokens * 3 * tokens * columns,
        2 * kept * tokens * 8 * columns,
    )(g, steps, mask, query, kv, low, high)
    if spans > 1:
        total = sums[groups].astype(bf16)
        members = [[s * groups + m for s in range(spans)] for m in range(groups)]
        totals = lax.all_gather(total, "tm", axis_index_groups=members).astype(jnp.float32)
        earlier = jnp.sum(
            jnp.where((jnp.arange(spans) < span)[:, None, None], totals, 0.0), axis=0
        )
        sums = [(v.astype(jnp.float32) + earlier[None]).astype(bf16) for v in sums[:groups]]
    sums = [sums[0]] + [swap(sums[s], "tm", s) for s in range(1, groups)]

    copies = groups * sum(len(blocks) for blocks in parts)
    return call(
        functools.partial(out_kernel, groups, parts),
        jax.ShapeDtypeStruct((steps_here, tokens, width), jnp.float32),
        [SMEM, VMEM] + [VMEM] * groups + [ANY] * (groups * len(parts)),
        VMEM,
        [pltpu.VMEM((groups, width, columns), bf16), pltpu.SemaphoreType.DMA((copies,))],
        2 * steps_here * tokens * width * width,
        2 * width * width + 6 * steps_here * tokens * width,
    )(where, start, *sums, *[v for slot in out_pieces for v in slot])


def solution(mesh):
    return jax.shard_map(
        body,
        mesh=mesh,
        in_specs=(
            P("tok", None),
            P("tm", "tok", None),
            P(),
            P("tok", None),
            P(),
            P("tok", None),
            P("tok", None),
        ),
        out_specs=P("tm", "tok", None),
        check_vma=False,
    )
```

```python
import functools
import math

import jax
import jax.numpy as jnp
from jax import lax
from jax.experimental import pallas as pl
from jax.experimental.pallas import tpu as pltpu
from jax.sharding import PartitionSpec as P

HEADS = 12
HEAD_DIM = 128
NSCHED = 1000
CORES = 2
VMEM_LIMIT = 28 * 1024 * 1024
KV_COST, Q_COST, ATT_COST, MOD_COST = 7, 20, 6, 30
CUT_LIMIT = 60 * 1024 * 1024
HBM = pl.BlockSpec(memory_space=pltpu.HBM)
VMEM = pl.BlockSpec(memory_space=pltpu.VMEM)
SMEM = pl.BlockSpec(memory_space=pltpu.SMEM)


def call(kernel, outs, in_specs, out_specs, scratch, cost, limit=VMEM_LIMIT):
    return pl.pallas_call(
        kernel,
        out_shape=outs,
        in_specs=in_specs,
        out_specs=out_specs,
        scratch_shapes=scratch,
        compiler_params=pltpu.CompilerParams(vmem_limit_bytes=limit),
        cost_estimate=pl.CostEstimate(flops=int(cost * 1_150_000_000), bytes_accessed=int(cost * 3_600_000), transcendentals=0),
    )


def head_groups(size):
    groups = 1
    while size % (2 * groups) == 0 and HEADS % (2 * groups) == 0:
        groups *= 2
    return groups


def swap(value, axis, mask):
    return lax.ppermute(value, axis, [(i, i ^ mask) for i in range(lax.axis_size(axis))])


def cut_kernel(g_ref, wqkv, wout, out, sems):
    width = wout.shape[1]
    columns = out.shape[1] // 4
    at = pl.multiple_of(g_ref[0] * columns, columns)
    sources = ((wqkv, width), (wqkv, 2 * width), (wqkv, 0), (wout, 0))
    copies = [
        (
            src.at[:, pl.ds(pl.multiple_of(base + at, columns), columns)],
            out.at[:, pl.ds(slot * columns, columns)],
        )
        for slot, (src, base) in enumerate(sources)
    ]
    for copy in start_all(copies, sems):
        copy.wait()


def keep_kernel(piece, out, sem):
    copy = pltpu.make_async_copy(piece, out, sem)
    copy.start()
    copy.wait()


def start_all(copies, sems):
    made = [pltpu.make_async_copy(src, dst, sems.at[n]) for n, (src, dst) in enumerate(copies)]
    for copy in made:
        copy.start()
    return made


def pack_kernel(at, where, *refs):
    pieces, (out, sems) = refs[:-2], refs[-2:]
    depth, columns = pieces[0].shape[0], out.shape[1]
    copies = [
        pltpu.make_async_copy(piece.at[:, pl.ds(at, columns)], out.at[pl.ds(min(n, 3) * depth, depth), :], sems.at[min(n, 3)])
        for n, piece in enumerate(pieces)
    ]
    for copy in copies[:3]:
        copy.start()

    @pl.when(where[0] == 1)
    def _():
        copies[3].start()

    @pl.when(where[0] != 1)
    def _():
        copies[4].start()

    for copy in copies[:4]:
        copy.wait()


def halves(value, axis):
    half = value.shape[axis] // 2
    return lax.slice_in_dim(value, 0, half, axis=axis), lax.slice_in_dim(value, half, None, axis=axis)


def modulate_kernel(act, weight, state, out):
    mod = jnp.dot(act[...], weight[...], preferred_element_type=jnp.float32)
    width = state.shape[-1]
    for i in range(state.shape[0]):
        values = state[i].astype(jnp.float32)
        center = values - jnp.mean(values, -1, keepdims=True)
        spread = jnp.mean(center * center, -1, keepdims=True)
        shift = mod[i : i + 1, :width]
        scale = mod[i : i + 1, width:]
        out[i] = (center / jnp.sqrt(spread + 1e-06) * (1.0 + scale) + shift).astype(jnp.bfloat16)


def head_norm(values):
    return values / jnp.sqrt(jnp.mean(values * values, -1, keepdims=True) + 1e-06)


def project_kernel(plan, where, *refs):
    states, pieces = refs[: plan["states"]], refs[plan["states"] : plan["states"] + plan["pieces"]]
    out, held, weight, sems = refs[plan["states"] + plan["pieces"] :]
    tokens, steps_here, kept, columns = plan["tokens"], plan["steps"], plan["kept"], plan["columns"]
    depth = pieces[0].shape[0]
    copies = []
    for n, piece in enumerate(pieces):
        row = where[1 + n]
        copies.append(
            (
                piece.at[:, pl.ds(columns[0], columns[1])],
                weight.at[pl.ds(pl.multiple_of(row * depth, depth), depth), :],
            )
        )
    for slot, state in enumerate(states):
        copies.append((state, held.at[pl.ds((where[0] ^ slot) * steps_here, steps_here)]))
    for copy in start_all(copies, sems):
        copy.wait()
    for slot in range(plan["groups"]):
        first = slot * steps_here
        count = min(steps_here, kept - first)
        rows = held[first : first + count].reshape(count * tokens, held.shape[-1])
        product = jnp.dot(rows, weight[: held.shape[-1], :], preferred_element_type=jnp.float32)
        for head in range(columns[1] // HEAD_DIM):
            cols = slice(head * HEAD_DIM, (head + 1) * HEAD_DIM)
            values = product[:, cols]
            if head < plan["normed"]:
                values = head_norm(values)
            out[first : first + count, :, cols] = values.astype(jnp.bfloat16).reshape(count, tokens, HEAD_DIM)


def attention_kernel(groups, steps_here, g_ref, steps, mask, query, near, own, far, *refs):
    outs, (total, before) = refs[:groups], refs[groups:]
    kept, tokens, columns = query.shape
    heads = columns // HEAD_DIM
    tiles = math.isqrt(mask.shape[0] // 3)
    size = tokens // tiles
    row_tile = lax.broadcasted_iota(jnp.int32, (tokens, 3 * tokens), 0) // size
    spot = row_tile * (3 * tiles) + lax.broadcasted_iota(jnp.int32, (tokens, 3 * tokens), 1) // size
    weights = jnp.zeros(spot.shape, jnp.float32)
    for n in range(mask.shape[0]):
        weights = jnp.where(spot == n, mask[n], weights)
    total[...] = jnp.zeros_like(total)
    before[0] = jnp.zeros(before.shape[1:], jnp.bfloat16)
    for k in range(kept):
        for head in range(heads):
            cols = slice(head * HEAD_DIM, (head + 1) * HEAD_DIM)
            vcols = slice(columns + head * HEAD_DIM, columns + (head + 1) * HEAD_DIM)
            keys = jnp.concatenate([near[k, :, cols], own[k, :, cols], far[k, :, cols]], axis=0)
            values = jnp.concatenate([near[k, :, vcols], own[k, :, vcols], far[k, :, vcols]], axis=0)
            score = lax.dot_general(
                query[k, :, cols],
                keys,
                (((1,), (1,)), ((), ())),
                preferred_element_type=jnp.float32,
            )
            expo = (jnp.exp2(score * (math.log2(math.e) / math.sqrt(HEAD_DIM))) * weights).astype(jnp.bfloat16)
            values = jnp.concatenate([values, jnp.ones_like(values)], axis=1)
            both = jnp.dot(expo, values, preferred_element_type=jnp.float32)
            attn = both[:, :HEAD_DIM] / both[:, HEAD_DIM:]
            total[:, cols] += steps[k] * attn.astype(jnp.bfloat16).astype(jnp.float32)
        before[k + 1] = total[...].astype(jnp.bfloat16)
    for slot, out in enumerate(outs):
        first = (g_ref[0] ^ slot) * steps_here
        for i in range(steps_here):
            out[i] = before[first + i]


def assemble_kernel(groups, blocks, where, *refs):
    pieces, (out, spare, sems) = refs[:-3], refs[-3:]
    columns = spare.shape[1]
    copies = []
    for slot in range(groups):
        cols = pl.ds(pl.multiple_of((where[0] ^ slot) * columns, columns), columns)
        for n, row, col, place, depth in blocks[slot]:
            source = pieces[n].at[pl.ds(row, depth), pl.ds(col, columns)]
            target = out.at[pl.ds(pl.multiple_of(where[1 + place] * depth, depth), depth), cols]
            copies.append((source, target, where[1 + place] * depth < out.shape[0]))
    for n, (source, target, used) in enumerate(copies):
        @pl.when(used)
        def _():
            pltpu.make_async_copy(source, target, sems.at[n]).start()
    for n, (source, target, used) in enumerate(copies):
        @pl.when(used)
        def _():
            pltpu.make_async_copy(source, target, sems.at[n]).wait()


def out_kernel(groups, where, start, weight, *refs):
    sums, (out,) = refs[:groups], refs[groups:]
    steps_here, tokens, columns = sums[0].shape
    rows = steps_here * tokens
    drift = jnp.zeros((rows, weight.shape[1]), jnp.float32)
    for slot in range(groups):
        place = pl.ds(pl.multiple_of((where[0] ^ slot) * columns, columns), columns)
        left = sums[slot][...].reshape(rows, columns)
        drift += jnp.dot(left, weight[place, :], preferred_element_type=jnp.float32)
    base = start[...].astype(jnp.float32)
    for i in range(steps_here):
        out[i] = base - drift[i * tokens : (i + 1) * tokens]


def body(start, trajectory, plan, neighbors, mod_weight, w_qkv, w_out):
    steps_here, tokens, width = trajectory.shape
    tm, tok = lax.axis_size("tm"), lax.axis_size("tok")
    groups = head_groups(tm)
    spans = tm // groups
    columns = width // groups
    depth = w_qkv.shape[0]
    index, place = lax.axis_index("tm"), lax.axis_index("tok")
    group, span = index % groups, index // groups
    chip, core = place // CORES, place % CORES
    count = groups * steps_here
    kept = count - 1 if spans == 1 else count
    bf16 = jnp.bfloat16
    g = group.astype(jnp.int32).reshape(1)

    mine = call(
        cut_kernel,
        jax.ShapeDtypeStruct((depth, 4 * columns), bf16),
        [SMEM, HBM, HBM],
        VMEM,
        [pltpu.SemaphoreType.DMA((4,))],
        2,
        CUT_LIMIT,
    )(g, w_qkv, w_out)
    trajectory, mine = lax.optimization_barrier((trajectory, mine))

    times = plan.astype(jnp.float32) / NSCHED
    own_times = lax.dynamic_slice_in_dim(times, index * steps_here, steps_here)
    span_times = lax.dynamic_slice_in_dim(times, span * count, count + 1)
    steps = span_times[:-1] - span_times[1:]
    half = mod_weight.shape[0] // 2
    freqs = jnp.exp(-math.log(10000.0) * jnp.arange(half, dtype=jnp.float32) / half)
    angle = 1000.0 * own_times[:, None] * freqs[None, :]
    embed = jnp.concatenate([jnp.cos(angle), jnp.sin(angle)], axis=1)
    act = jnp.pad(jax.nn.silu(embed).astype(bf16), ((0, -steps_here % 16), (0, 0)))
    normed = call(
        modulate_kernel,
        jax.ShapeDtypeStruct(trajectory.shape, bf16),
        [VMEM] * 3,
        VMEM,
        [],
        MOD_COST,
    )(act, mod_weight, trajectory)

    tiles = neighbors.shape[0]
    tile = tokens // tiles
    local = neighbors - tiles * (place - 1)
    times_listed = jnp.sum(
        (local[:, :, None] == jnp.arange(3 * tiles, dtype=jnp.int32)).astype(jnp.float32), axis=1
    )
    sides = times_listed.reshape(tiles, 3, tiles)
    sides = jnp.where(place % 2 == 0, sides[:, ::-1], sides).reshape(tiles, 3 * tiles)
    mask = sides.reshape(-1)

    states = [normed] + [swap(normed, "tm", s) for s in range(1, groups)]
    on_line = tok == 4 * CORES and groups == 4
    if on_line:
        inside = [(c * CORES + p, (c ^ 3) * CORES + p) for c in (1, 2) for p in range(CORES)]
        relays = [(c * CORES + p, (c ^ 1) * CORES + p) for c in (1, 2) for p in range(CORES)]
        inner = ((chip > 0) & (chip < 3)).astype(jnp.int32)
        spare = jnp.full((), tok, jnp.int32)
        last = [jnp.where(inner == 1, chip ^ 3, spare), jnp.where(inner == 1, spare, chip ^ 3)]
        chips = [chip, chip ^ 2, chip ^ 1] + last
        rows = [jnp.where(c == spare, spare, c * CORES + q) for q in (core, 1 - core) for c in chips]
        line_rows = [(chip ^ m) * CORES + q for q in (core, 1 - core) for m in (0, 2, 1, 3)]
        where = jnp.stack([group] + rows).astype(jnp.int32)
        block_rows = jnp.stack([group] + rows + line_rows).astype(jnp.int32)
        inner = inner.reshape(1)
        own = call(
            keep_kernel,
            jax.ShapeDtypeStruct(mine.shape, bf16),
            [HBM],
            VMEM,
            [pltpu.SemaphoreType.DMA],
            2,
        )(mine)
        own, mine, far, near, where, block_rows, inner, mask, steps = lax.optimization_barrier(
            (
                own,
                mine,
                swap(mine, "tok", 2 * CORES),
                swap(mine, "tok", CORES),
                where,
                block_rows,
                inner,
                mask,
                steps,
            )
        )
        middle, relayed = lax.ppermute(mine, "tok", inside), lax.ppermute(far, "tok", relays)
        line = [own, far, near, middle, relayed]
        pieces = line + [swap(v, "tok", 1) for v in line]
    else:
        pieces = [lax.all_gather(mine, "tok", axis=0, tiled=True)]
        where = block_rows = jnp.stack([group, jnp.zeros_like(group)]).astype(jnp.int32)
    depths = pieces[0].shape[0]
    held_rows = width + (depths if on_line else 0)

    def project(states, cols, normed_heads, cost):
        info = {
            "states": len(states),
            "groups": groups,
            "pieces": len(pieces),
            "tokens": tokens,
            "steps": steps_here,
            "kept": kept,
            "columns": cols,
            "normed": normed_heads,
        }
        return call(
            functools.partial(project_kernel, info),
            jax.ShapeDtypeStruct((kept, tokens, cols[1]), bf16),
            [SMEM] + [HBM] * (len(states) + len(pieces)),
            VMEM,
            [
                pltpu.VMEM((count, tokens, width), bf16),
                pltpu.VMEM((held_rows, cols[1]), bf16),
                pltpu.SemaphoreType.DMA((len(states) + len(pieces),)),
            ],
            cost,
        )(where, *states, *pieces)

    if on_line:
        packed = call(
            functools.partial(pack_kernel, 3 * columns),
            jax.ShapeDtypeStruct((4 * depth, columns), bf16),
            [SMEM] + [HBM] * 5,
            VMEM,
            [pltpu.SemaphoreType.DMA((4,))],
            2,
        )(inner, *line)
        states, packed = lax.optimization_barrier((states, packed))
        beside, across = swap(packed, "tm", 1), swap(packed, "tm", 2)
        others = [beside, across, swap(halves(beside, 0)[0], "tm", 2), swap(halves(across, 0)[1], "tm", 1)]
        blocks = [[(n, 0, 3 * columns, n, depth) for n in range(10)]]
        for slot in range(2):
            blocks.append([(10 + slot + 4 * (n // 4), n % 4 * depth, 0, 10 + n, depth) for n in range(8)])
        blocks.append([(12 + n // 2 % 2 + 4 * (n // 4), n % 2 * depth, 0, 10 + n, depth) for n in range(8)])
    else:
        whole = pieces[0][:, 3 * columns :]
        out_pieces = [whole] + [swap(whole, "tm", s) for s in range(1, groups)]
        blocks = [[(slot, 0, 0, 0, width)] for slot in range(groups)]

    heads = columns // HEAD_DIM
    kv = project(states, (0, 2 * columns), heads, KV_COST)
    far_kv = lax.ppermute(kv, "tok", [(i, ((i + 1) ^ 1) - 1) for i in range(1, tok - 1)])
    near_kv = swap(kv, "tok", 1)
    states_after, _ = lax.optimization_barrier((states, kv))
    query = project(states_after, (2 * columns, columns), heads, Q_COST)
    summed = jax.ShapeDtypeStruct((steps_here, tokens, columns), bf16)
    sums = call(
        functools.partial(attention_kernel, groups, steps_here),
        [summed] * groups + ([] if spans == 1 else [jax.ShapeDtypeStruct((tokens, columns), jnp.float32)]),
        [SMEM] * 3 + [VMEM] * 4,
        [VMEM] * (groups if spans == 1 else groups + 1),
        ([pltpu.VMEM((tokens, columns), jnp.float32)] if spans == 1 else [])
        + [
            pltpu.VMEM((kept + 1, tokens, columns), bf16),
        ],
        ATT_COST,
    )(g, steps, mask, query, near_kv, kv, far_kv)
    if spans > 1:
        total = sums[groups].astype(bf16)
        members = [[s * groups + m for s in range(spans)] for m in range(groups)]
        totals = lax.all_gather(total, "tm", axis_index_groups=members).astype(jnp.float32)
        earlier = jnp.sum(
            jnp.where((jnp.arange(spans) < span)[:, None, None], totals, 0.0), axis=0
        )
        sums = [(v.astype(jnp.float32) + earlier[None]).astype(bf16) for v in sums[:groups]]
    if on_line:
        out_pieces = pieces + others + [swap(v, "tok", 1) for v in others]
    sums = [sums[0]] + [swap(sums[s], "tm", s) for s in range(1, groups)]

    weight = call(
        functools.partial(assemble_kernel, groups, blocks),
        jax.ShapeDtypeStruct((width, width), bf16),
        [SMEM] + [HBM] * len(out_pieces),
        VMEM,
        [pltpu.VMEM((8, columns), bf16), pltpu.SemaphoreType.DMA((sum(len(each) for each in blocks),))],
        4,
    )(block_rows, *out_pieces)
    return call(
        functools.partial(out_kernel, groups),
        jax.ShapeDtypeStruct((steps_here, tokens, width), jnp.float32),
        [SMEM] + [VMEM] * (2 + groups),
        VMEM,
        [],
        4,
    )(g, start, weight, *sums)


def solution(mesh):
    return jax.shard_map(
        body,
        mesh=mesh,
        in_specs=(
            P("tok", None),
            P("tm", "tok", None),
            P(),
            P("tok", None),
            P(),
            P("tok", None),
            P("tok", None),
        ),
        out_specs=P("tm", "tok", None),
        check_vma=False,
    )
```

```python
import functools
import math

import jax
import jax.numpy as jnp
from jax import lax
from jax.experimental import pallas as pl
from jax.experimental.pallas import tpu as pltpu
from jax.sharding import PartitionSpec as P

HEADS = 12
HEAD_DIM = 128
NSCHED = 1000
CORES = 2
VMEM_LIMIT = 28 * 1024 * 1024
KV_COST, Q_COST, ATT_COST, MOD_COST = 7, 20, 6, 30
CUT_LIMIT = 60 * 1024 * 1024
HBM = pl.BlockSpec(memory_space=pltpu.HBM)
VMEM = pl.BlockSpec(memory_space=pltpu.VMEM)
SMEM = pl.BlockSpec(memory_space=pltpu.SMEM)


def call(kernel, outs, in_specs, out_specs, scratch, cost, limit=VMEM_LIMIT):
    return pl.pallas_call(
        kernel,
        out_shape=outs,
        in_specs=in_specs,
        out_specs=out_specs,
        scratch_shapes=scratch,
        compiler_params=pltpu.CompilerParams(vmem_limit_bytes=limit),
        cost_estimate=pl.CostEstimate(flops=int(cost * 1_150_000_000), bytes_accessed=int(cost * 3_600_000), transcendentals=0),
    )


def head_groups(size):
    groups = 1
    while size % (2 * groups) == 0 and HEADS % (2 * groups) == 0:
        groups *= 2
    return groups


def swap(value, axis, mask):
    return lax.ppermute(value, axis, [(i, i ^ mask) for i in range(lax.axis_size(axis))])


def cut_kernel(g_ref, wqkv, wout, out, sems):
    width = wout.shape[1]
    columns = out.shape[1] // 4
    at = pl.multiple_of(g_ref[0] * columns, columns)
    sources = ((wqkv, width), (wqkv, 2 * width), (wqkv, 0), (wout, 0))
    copies = [
        (
            src.at[:, pl.ds(pl.multiple_of(base + at, columns), columns)],
            out.at[:, pl.ds(slot * columns, columns)],
        )
        for slot, (src, base) in enumerate(sources)
    ]
    for copy in start_all(copies, sems):
        copy.wait()


def keep_kernel(*refs):
    count = len(refs) // 2
    for copy in start_all([(refs[n], refs[count + n]) for n in range(count)], refs[-1]):
        copy.wait()


def start_all(copies, sems):
    made = [pltpu.make_async_copy(src, dst, sems.at[n]) for n, (src, dst) in enumerate(copies)]
    for copy in made:
        copy.start()
    return made


def pack_kernel(at, where, *refs):
    pieces, (out, sems) = refs[:-2], refs[-2:]
    depth, columns = pieces[0].shape[0], out.shape[1]
    copies = [
        pltpu.make_async_copy(piece.at[:, pl.ds(at, columns)], out.at[pl.ds(min(n, 3) * depth, depth), :], sems.at[min(n, 3)])
        for n, piece in enumerate(pieces)
    ]
    for copy in copies[:3]:
        copy.start()

    @pl.when(where[0] == 1)
    def _():
        copies[3].start()

    @pl.when(where[0] != 1)
    def _():
        copies[4].start()

    for copy in copies[:4]:
        copy.wait()


def halves(value, axis):
    half = value.shape[axis] // 2
    return lax.slice_in_dim(value, 0, half, axis=axis), lax.slice_in_dim(value, half, None, axis=axis)


def modulate_kernel(act, weight, state, out):
    mod = jnp.dot(act[...], weight[...], preferred_element_type=jnp.float32)
    width = state.shape[-1]
    for i in range(state.shape[0]):
        values = state[i].astype(jnp.float32)
        center = values - jnp.mean(values, -1, keepdims=True)
        spread = jnp.mean(center * center, -1, keepdims=True)
        shift = mod[i : i + 1, :width]
        scale = mod[i : i + 1, width:]
        out[i] = (center / jnp.sqrt(spread + 1e-06) * (1.0 + scale) + shift).astype(jnp.bfloat16)


def head_norm(values):
    return values / jnp.sqrt(jnp.mean(values * values, -1, keepdims=True) + 1e-06)


def project_kernel(plan, where, *refs):
    states, pieces = refs[: plan["states"]], refs[plan["states"] : plan["states"] + plan["pieces"]]
    out, every, weight, sems = refs[plan["states"] + plan["pieces"] :]
    tokens, steps_here, kept, columns = plan["tokens"], plan["steps"], plan["kept"], plan["columns"]
    depth = pieces[0].shape[0]
    copies = []
    for n, piece in enumerate(pieces):
        row = where[1 + n]
        copies.append(
            (
                piece.at[:, pl.ds(columns[0], columns[1])],
                weight.at[pl.ds(pl.multiple_of(row * depth, depth), depth), :],
            )
        )
    for copy in start_all(copies, sems):
        copy.wait()

    for state, (slot, begin) in zip(states, plan["places"]):
        count, _, width = state.shape
        first = (where[0] ^ slot) * steps_here + begin
        rows = state[...].reshape(count * tokens, width)
        product = jnp.dot(rows, weight[:width, :], preferred_element_type=jnp.float32)
        for head in range(columns[1] // HEAD_DIM):
            cols = slice(head * HEAD_DIM, (head + 1) * HEAD_DIM)
            values = product[:, cols]
            if head < plan["normed"]:
                values = head_norm(values)
            values = values.astype(jnp.bfloat16).reshape(count, tokens, HEAD_DIM)
            every[pl.ds(first, count), :, cols] = values
    out[...] = every[:kept]


def attention_kernel(groups, steps_here, g_ref, steps, mask, query, near, own, far, *refs):
    outs, (total, before) = refs[:groups], refs[groups:]
    kept, tokens, columns = query.shape
    heads = columns // HEAD_DIM
    tiles = math.isqrt(mask.shape[0] // 3)
    size = tokens // tiles
    row_tile = lax.broadcasted_iota(jnp.int32, (tokens, 3 * tokens), 0) // size
    spot = row_tile * (3 * tiles) + lax.broadcasted_iota(jnp.int32, (tokens, 3 * tokens), 1) // size
    weights = jnp.zeros(spot.shape, jnp.float32)
    for n in range(mask.shape[0]):
        weights = jnp.where(spot == n, mask[n], weights)
    total[...] = jnp.zeros_like(total)
    before[0] = jnp.zeros(before.shape[1:], jnp.bfloat16)
    for k in range(kept):
        for head in range(heads):
            cols = slice(head * HEAD_DIM, (head + 1) * HEAD_DIM)
            vcols = slice(columns + head * HEAD_DIM, columns + (head + 1) * HEAD_DIM)
            keys = jnp.concatenate([near[k, :, cols], own[k, :, cols], far[k, :, cols]], axis=0)
            values = jnp.concatenate([near[k, :, vcols], own[k, :, vcols], far[k, :, vcols]], axis=0)
            score = lax.dot_general(
                query[k, :, cols],
                keys,
                (((1,), (1,)), ((), ())),
                preferred_element_type=jnp.float32,
            )
            expo = (jnp.exp2(score * (math.log2(math.e) / math.sqrt(HEAD_DIM))) * weights).astype(jnp.bfloat16)
            values = jnp.concatenate([values, jnp.ones_like(values)], axis=1)
            both = jnp.dot(expo, values, preferred_element_type=jnp.float32)
            attn = both[:, :HEAD_DIM] / both[:, HEAD_DIM:]
            total[:, cols] += steps[k] * attn.astype(jnp.bfloat16).astype(jnp.float32)
        before[k + 1] = total[...].astype(jnp.bfloat16)
    for slot, out in enumerate(outs):
        first = (g_ref[0] ^ slot) * steps_here
        for i in range(steps_here):
            out[i] = before[first + i]


def assemble_kernel(groups, blocks, where, *refs):
    pieces, (out, spare, sems) = refs[:-3], refs[-3:]
    columns = spare.shape[1]
    copies = []
    for slot in range(groups):
        cols = pl.ds(pl.multiple_of((where[0] ^ slot) * columns, columns), columns)
        for n, row, col, place, depth in blocks[slot]:
            source = pieces[n].at[pl.ds(row, depth), pl.ds(col, columns)]
            target = out.at[pl.ds(pl.multiple_of(where[1 + place] * depth, depth), depth), cols]
            copies.append((source, target, where[1 + place] * depth < out.shape[0]))
    for n, (source, target, used) in enumerate(copies):
        @pl.when(used)
        def _():
            pltpu.make_async_copy(source, target, sems.at[n]).start()
    for n, (source, target, used) in enumerate(copies):
        @pl.when(used)
        def _():
            pltpu.make_async_copy(source, target, sems.at[n]).wait()


def out_kernel(groups, where, start, weight, *refs):
    sums, (out,) = refs[:groups], refs[groups:]
    steps_here, tokens, columns = sums[0].shape
    rows = steps_here * tokens
    drift = jnp.zeros((rows, weight.shape[1]), jnp.float32)
    for slot in range(groups):
        place = pl.ds(pl.multiple_of((where[0] ^ slot) * columns, columns), columns)
        left = sums[slot][...].reshape(rows, columns)
        drift += jnp.dot(left, weight[place, :], preferred_element_type=jnp.float32)
    base = start[...].astype(jnp.float32)
    for i in range(steps_here):
        out[i] = base - drift[i * tokens : (i + 1) * tokens]


def body(start, trajectory, plan, neighbors, mod_weight, w_qkv, w_out):
    steps_here, tokens, width = trajectory.shape
    tm, tok = lax.axis_size("tm"), lax.axis_size("tok")
    groups = head_groups(tm)
    spans = tm // groups
    columns = width // groups
    depth = w_qkv.shape[0]
    index, place = lax.axis_index("tm"), lax.axis_index("tok")
    group, span = index % groups, index // groups
    chip, core = place // CORES, place % CORES
    count = groups * steps_here
    kept = count - 1 if spans == 1 else count
    bf16 = jnp.bfloat16
    g = group.astype(jnp.int32).reshape(1)

    mine = call(
        cut_kernel,
        jax.ShapeDtypeStruct((depth, 4 * columns), bf16),
        [SMEM, HBM, HBM],
        VMEM,
        [pltpu.SemaphoreType.DMA((4,))],
        2,
        CUT_LIMIT,
    )(g, w_qkv, w_out)
    trajectory, mine = lax.optimization_barrier((trajectory, mine))

    times = plan.astype(jnp.float32) / NSCHED
    own_times = lax.dynamic_slice_in_dim(times, index * steps_here, steps_here)
    span_times = lax.dynamic_slice_in_dim(times, span * count, count + 1)
    steps = span_times[:-1] - span_times[1:]
    half = mod_weight.shape[0] // 2
    freqs = jnp.exp(-math.log(10000.0) * jnp.arange(half, dtype=jnp.float32) / half)
    angle = 1000.0 * own_times[:, None] * freqs[None, :]
    embed = jnp.concatenate([jnp.cos(angle), jnp.sin(angle)], axis=1)
    act = jnp.pad(jax.nn.silu(embed).astype(bf16), ((0, -steps_here % 16), (0, 0)))
    normed = call(
        modulate_kernel,
        jax.ShapeDtypeStruct(trajectory.shape, bf16),
        [VMEM] * 3,
        VMEM,
        [],
        MOD_COST,
    )(act, mod_weight, trajectory)

    tiles = neighbors.shape[0]
    tile = tokens // tiles
    local = neighbors - tiles * (place - 1)
    times_listed = jnp.sum(
        (local[:, :, None] == jnp.arange(3 * tiles, dtype=jnp.int32)).astype(jnp.float32), axis=1
    )
    sides = times_listed.reshape(tiles, 3, tiles)
    sides = jnp.where(place % 2 == 0, sides[:, ::-1], sides).reshape(tiles, 3 * tiles)
    mask = sides.reshape(-1)

    on_line = tok == 4 * CORES and groups == 4
    if on_line:
        inside = [(c * CORES + p, (c ^ 3) * CORES + p) for c in (1, 2) for p in range(CORES)]
        relays = [(c * CORES + p, (c ^ 1) * CORES + p) for c in (1, 2) for p in range(CORES)]
        inner = ((chip > 0) & (chip < 3)).astype(jnp.int32)
        spare = jnp.full((), tok, jnp.int32)
        last = [jnp.where(inner == 1, chip ^ 3, spare), jnp.where(inner == 1, spare, chip ^ 3)]
        chips = [chip, chip ^ 2, chip ^ 1] + last
        rows = [jnp.where(c == spare, spare, c * CORES + q) for q in (core, 1 - core) for c in chips]
        line_rows = [(chip ^ m) * CORES + q for q in (core, 1 - core) for m in (0, 2, 1, 3)]
        where = jnp.stack([group] + rows).astype(jnp.int32)
        block_rows = jnp.stack([group] + rows + line_rows).astype(jnp.int32)
        inner = inner.reshape(1)
        mine, far, near, where, block_rows, inner, mask, steps = lax.optimization_barrier(
            (
                mine,
                swap(mine, "tok", 2 * CORES),
                swap(mine, "tok", CORES),
                where,
                block_rows,
                inner,
                mask,
                steps,
            )
        )
        states = [normed] + [swap(normed, "tm", s) for s in range(1, groups)]
        places = [(s, 0) for s in range(groups)]
        middle, relayed = lax.ppermute(mine, "tok", inside), lax.ppermute(far, "tok", relays)
        kept_line = call(
            keep_kernel,
            [jax.ShapeDtypeStruct(mine.shape, bf16)] * 3,
            [HBM] * 3,
            [VMEM] * 3,
            [pltpu.SemaphoreType.DMA((3,))],
            2,
        )(mine, far, near)
        line = list(kept_line) + [middle, relayed]
        pieces = line + [swap(v, "tok", 1) for v in line]
    else:
        states = [normed] + [swap(normed, "tm", s) for s in range(1, groups)]
        places = [(s, 0) for s in range(groups)]
        pieces = [lax.all_gather(mine, "tok", axis=0, tiled=True)]
        where = block_rows = jnp.stack([group, jnp.zeros_like(group)]).astype(jnp.int32)
    depths = pieces[0].shape[0]
    held_rows = width + (depths if on_line else 0)

    def project(states, cols, normed_heads, cost):
        info = {
            "states": len(states),
            "groups": groups,
            "places": places,
            "pieces": len(pieces),
            "tokens": tokens,
            "steps": steps_here,
            "kept": kept,
            "columns": cols,
            "normed": normed_heads,
        }
        return call(
            functools.partial(project_kernel, info),
            jax.ShapeDtypeStruct((kept, tokens, cols[1]), bf16),
            [SMEM] + [VMEM] * len(states) + [HBM] * len(pieces),
            VMEM,
            [
                pltpu.VMEM((count, tokens, cols[1]), bf16),
                pltpu.VMEM((held_rows, cols[1]), bf16),
                pltpu.SemaphoreType.DMA((len(pieces),)),
            ],
            cost,
        )(where, *states, *pieces)

    if on_line:
        packed = call(
            functools.partial(pack_kernel, 3 * columns),
            jax.ShapeDtypeStruct((4 * depth, columns), bf16),
            [SMEM] + [HBM] * 5,
            VMEM,
            [pltpu.SemaphoreType.DMA((4,))],
            2,
        )(inner, *line)
        states, packed = lax.optimization_barrier((states, packed))
        beside, across = swap(packed, "tm", 1), swap(packed, "tm", 2)
        others = [beside, across, swap(halves(beside, 0)[0], "tm", 2), swap(halves(across, 0)[1], "tm", 1)]
        blocks = [[(n, 0, 3 * columns, n, depth) for n in range(10)]]
        for slot in range(2):
            blocks.append([(10 + slot + 4 * (n // 4), n % 4 * depth, 0, 10 + n, depth) for n in range(8)])
        blocks.append([(12 + n // 2 % 2 + 4 * (n // 4), n % 2 * depth, 0, 10 + n, depth) for n in range(8)])
    else:
        whole = pieces[0][:, 3 * columns :]
        out_pieces = [whole] + [swap(whole, "tm", s) for s in range(1, groups)]
        blocks = [[(slot, 0, 0, 0, width)] for slot in range(groups)]

    heads = columns // HEAD_DIM
    kv = project(states, (0, 2 * columns), heads, KV_COST)
    far_kv = lax.ppermute(kv, "tok", [(i, ((i + 1) ^ 1) - 1) for i in range(1, tok - 1)])
    near_kv = swap(kv, "tok", 1)
    states_after, _ = lax.optimization_barrier((states, kv))
    query = project(states_after, (2 * columns, columns), heads, Q_COST)
    summed = jax.ShapeDtypeStruct((steps_here, tokens, columns), bf16)
    sums = call(
        functools.partial(attention_kernel, groups, steps_here),
        [summed] * groups + ([] if spans == 1 else [jax.ShapeDtypeStruct((tokens, columns), jnp.float32)]),
        [SMEM] * 3 + [VMEM] * 4,
        [VMEM] * (groups if spans == 1 else groups + 1),
        ([pltpu.VMEM((tokens, columns), jnp.float32)] if spans == 1 else [])
        + [
            pltpu.VMEM((kept + 1, tokens, columns), bf16),
        ],
        ATT_COST,
    )(g, steps, mask, query, near_kv, kv, far_kv)
    if spans > 1:
        total = sums[groups].astype(bf16)
        members = [[s * groups + m for s in range(spans)] for m in range(groups)]
        totals = lax.all_gather(total, "tm", axis_index_groups=members).astype(jnp.float32)
        earlier = jnp.sum(
            jnp.where((jnp.arange(spans) < span)[:, None, None], totals, 0.0), axis=0
        )
        sums = [(v.astype(jnp.float32) + earlier[None]).astype(bf16) for v in sums[:groups]]
    if on_line:
        out_pieces = pieces + others + [swap(v, "tok", 1) for v in others]
    sums = [sums[0]] + [swap(sums[s], "tm", s) for s in range(1, groups)]

    weight = call(
        functools.partial(assemble_kernel, groups, blocks),
        jax.ShapeDtypeStruct((width, width), bf16),
        [SMEM] + [HBM] * len(out_pieces),
        VMEM,
        [pltpu.VMEM((8, columns), bf16), pltpu.SemaphoreType.DMA((sum(len(each) for each in blocks),))],
        4,
    )(block_rows, *out_pieces)
    return call(
        functools.partial(out_kernel, groups),
        jax.ShapeDtypeStruct((steps_here, tokens, width), jnp.float32),
        [SMEM] + [VMEM] * (2 + groups),
        VMEM,
        [],
        4,
    )(g, start, weight, *sums)


def solution(mesh):
    return jax.shard_map(
        body,
        mesh=mesh,
        in_specs=(
            P("tok", None),
            P("tm", "tok", None),
            P(),
            P("tok", None),
            P(),
            P("tok", None),
            P("tok", None),
        ),
        out_specs=P("tm", "tok", None),
        check_vma=False,
    )
```

```python
import functools
import math

import jax
import jax.numpy as jnp
from jax import lax
from jax.experimental import pallas as pl
from jax.experimental.pallas import tpu as pltpu
from jax.sharding import PartitionSpec as P

HEADS = 12
HEAD_DIM = 128
NSCHED = 1000
CORES = 2
VMEM_LIMIT = 28 * 1024 * 1024
KV_COST, Q_COST, ATT_COST, MOD_COST = 7, 20, 6, 30
HBM = pl.BlockSpec(memory_space=pltpu.HBM)
VMEM = pl.BlockSpec(memory_space=pltpu.VMEM)
SMEM = pl.BlockSpec(memory_space=pltpu.SMEM)


def call(kernel, outs, in_specs, out_specs, scratch, cost, limit=VMEM_LIMIT):
    return pl.pallas_call(
        kernel,
        out_shape=outs,
        in_specs=in_specs,
        out_specs=out_specs,
        scratch_shapes=scratch,
        compiler_params=pltpu.CompilerParams(vmem_limit_bytes=limit),
        cost_estimate=pl.CostEstimate(flops=int(cost * 1_150_000_000), bytes_accessed=int(cost * 3_600_000), transcendentals=0),
    )


def head_groups(size):
    groups = 1
    while size % (2 * groups) == 0 and HEADS % (2 * groups) == 0:
        groups *= 2
    return groups


def swap(value, axis, mask):
    return lax.ppermute(value, axis, [(i, i ^ mask) for i in range(lax.axis_size(axis))])


def keep_kernel(*refs):
    count = len(refs) // 2
    for copy in start_all([(refs[n], refs[count + n]) for n in range(count)], refs[-1]):
        copy.wait()


def start_all(copies, sems):
    made = [pltpu.make_async_copy(src, dst, sems.at[n]) for n, (src, dst) in enumerate(copies)]
    for copy in made:
        copy.start()
    return made


def pack_kernel(at, where, *refs):
    pieces, (out, sems) = refs[:-2], refs[-2:]
    depth, columns = pieces[0].shape[0], out.shape[1]
    copies = [
        pltpu.make_async_copy(piece.at[:, pl.ds(at, columns)], out.at[pl.ds(min(n, 3) * depth, depth), :], sems.at[min(n, 3)])
        for n, piece in enumerate(pieces)
    ]
    for copy in copies[:3]:
        copy.start()

    @pl.when(where[0] == 1)
    def _():
        copies[3].start()

    @pl.when(where[0] != 1)
    def _():
        copies[4].start()

    for copy in copies[:4]:
        copy.wait()


def halves(value, axis):
    half = value.shape[axis] // 2
    return lax.slice_in_dim(value, 0, half, axis=axis), lax.slice_in_dim(value, half, None, axis=axis)


def modulate_kernel(act, weight, state, out):
    mod = jnp.dot(act[...], weight[...], preferred_element_type=jnp.float32)
    width = state.shape[-1]
    for i in range(state.shape[0]):
        values = state[i].astype(jnp.float32)
        center = values - jnp.mean(values, -1, keepdims=True)
        spread = jnp.mean(center * center, -1, keepdims=True)
        shift = mod[i : i + 1, :width]
        scale = mod[i : i + 1, width:]
        out[i] = (center / jnp.sqrt(spread + 1e-06) * (1.0 + scale) + shift).astype(jnp.bfloat16)


def head_norm(values):
    return values / jnp.sqrt(jnp.mean(values * values, -1, keepdims=True) + 1e-06)


def project_kernel(plan, where, *refs):
    states, pieces = refs[: plan["states"]], refs[plan["states"] : plan["states"] + plan["pieces"]]
    out, every, weight, sems = refs[plan["states"] + plan["pieces"] :]
    tokens, steps_here, kept, columns = plan["tokens"], plan["steps"], plan["kept"], plan["columns"]
    depth = pieces[0].shape[0]
    copies = []
    for n, piece in enumerate(pieces):
        row = where[1 + n]
        copies.append(
            (
                piece.at[:, pl.ds(columns[0], columns[1])],
                weight.at[pl.ds(pl.multiple_of(row * depth, depth), depth), :],
            )
        )
    for copy in start_all(copies, sems):
        copy.wait()

    for state, (slot, begin) in zip(states, plan["places"]):
        count, _, width = state.shape
        first = (where[0] ^ slot) * steps_here + begin
        rows = state[...].reshape(count * tokens, width)
        product = jnp.dot(rows, weight[:width, :], preferred_element_type=jnp.float32)
        for head in range(columns[1] // HEAD_DIM):
            cols = slice(head * HEAD_DIM, (head + 1) * HEAD_DIM)
            values = product[:, cols]
            if head < plan["normed"]:
                values = head_norm(values)
            values = values.astype(jnp.bfloat16).reshape(count, tokens, HEAD_DIM)
            every[pl.ds(first, count), :, cols] = values
    out[...] = every[:kept]


def attention_kernel(groups, steps_here, g_ref, steps, mask, query, near, own, far, *refs):
    outs, (total, before) = refs[:groups], refs[groups:]
    kept, tokens, columns = query.shape
    heads = columns // HEAD_DIM
    tiles = math.isqrt(mask.shape[0] // 3)
    size = tokens // tiles
    row_tile = lax.broadcasted_iota(jnp.int32, (tokens, 3 * tokens), 0) // size
    spot = row_tile * (3 * tiles) + lax.broadcasted_iota(jnp.int32, (tokens, 3 * tokens), 1) // size
    weights = jnp.zeros(spot.shape, jnp.float32)
    for n in range(mask.shape[0]):
        weights = jnp.where(spot == n, mask[n], weights)
    total[...] = jnp.zeros_like(total)
    before[0] = jnp.zeros(before.shape[1:], jnp.bfloat16)
    for k in range(kept):
        for head in range(heads):
            cols = slice(head * HEAD_DIM, (head + 1) * HEAD_DIM)
            vcols = slice(columns + head * HEAD_DIM, columns + (head + 1) * HEAD_DIM)
            keys = jnp.concatenate([near[k, :, cols], own[k, :, cols], far[k, :, cols]], axis=0)
            values = jnp.concatenate([near[k, :, vcols], own[k, :, vcols], far[k, :, vcols]], axis=0)
            score = lax.dot_general(
                query[k, :, cols],
                keys,
                (((1,), (1,)), ((), ())),
                preferred_element_type=jnp.float32,
            )
            expo = (jnp.exp2(score * (math.log2(math.e) / math.sqrt(HEAD_DIM))) * weights).astype(jnp.bfloat16)
            values = jnp.concatenate([values, jnp.ones_like(values)], axis=1)
            both = jnp.dot(expo, values, preferred_element_type=jnp.float32)
            attn = both[:, :HEAD_DIM] / both[:, HEAD_DIM:]
            total[:, cols] += steps[k] * attn.astype(jnp.bfloat16).astype(jnp.float32)
        before[k + 1] = total[...].astype(jnp.bfloat16)
    for slot, out in enumerate(outs):
        first = (g_ref[0] ^ slot) * steps_here
        for i in range(steps_here):
            out[i] = before[first + i]


def assemble_kernel(groups, blocks, where, *refs):
    pieces, (out, spare, sems) = refs[:-3], refs[-3:]
    columns = spare.shape[1]
    copies = []
    for slot in range(groups):
        cols = pl.ds(pl.multiple_of((where[0] ^ slot) * columns, columns), columns)
        for n, row, col, place, depth in blocks[slot]:
            source = pieces[n].at[pl.ds(row, depth), pl.ds(col, columns)]
            target = out.at[pl.ds(pl.multiple_of(where[1 + place] * depth, depth), depth), cols]
            copies.append((source, target, where[1 + place] * depth < out.shape[0]))
    for n, (source, target, used) in enumerate(copies):
        @pl.when(used)
        def _():
            pltpu.make_async_copy(source, target, sems.at[n]).start()
    for n, (source, target, used) in enumerate(copies):
        @pl.when(used)
        def _():
            pltpu.make_async_copy(source, target, sems.at[n]).wait()


def out_kernel(groups, where, start, weight, *refs):
    sums, (out,) = refs[:groups], refs[groups:]
    steps_here, tokens, columns = sums[0].shape
    rows = steps_here * tokens
    drift = jnp.zeros((rows, weight.shape[1]), jnp.float32)
    for slot in range(groups):
        place = pl.ds(pl.multiple_of((where[0] ^ slot) * columns, columns), columns)
        left = sums[slot][...].reshape(rows, columns)
        drift += jnp.dot(left, weight[place, :], preferred_element_type=jnp.float32)
    base = start[...].astype(jnp.float32)
    for i in range(steps_here):
        out[i] = base - drift[i * tokens : (i + 1) * tokens]


def body(start, trajectory, plan, neighbors, mod_weight, w_qkv, w_out):
    steps_here, tokens, width = trajectory.shape
    tm, tok = lax.axis_size("tm"), lax.axis_size("tok")
    groups = head_groups(tm)
    spans = tm // groups
    columns = width // groups
    depth = w_qkv.shape[0]
    index, place = lax.axis_index("tm"), lax.axis_index("tok")
    group, span = index % groups, index // groups
    chip, core = place // CORES, place % CORES
    count = groups * steps_here
    kept = count - 1 if spans == 1 else count
    bf16 = jnp.bfloat16
    g = group.astype(jnp.int32).reshape(1)

    at = group * columns
    mine = jnp.concatenate(
        [
            lax.dynamic_slice_in_dim(w_qkv, width + at, columns, axis=1),
            lax.dynamic_slice_in_dim(w_qkv, 2 * width + at, columns, axis=1),
            lax.dynamic_slice_in_dim(w_qkv, at, columns, axis=1),
            lax.dynamic_slice_in_dim(w_out, at, columns, axis=1),
        ],
        axis=1,
    )
    trajectory, mine = lax.optimization_barrier((trajectory, mine))

    times = plan.astype(jnp.float32) / NSCHED
    own_times = lax.dynamic_slice_in_dim(times, index * steps_here, steps_here)
    span_times = lax.dynamic_slice_in_dim(times, span * count, count + 1)
    steps = span_times[:-1] - span_times[1:]
    half = mod_weight.shape[0] // 2
    freqs = jnp.exp(-math.log(10000.0) * jnp.arange(half, dtype=jnp.float32) / half)
    angle = 1000.0 * own_times[:, None] * freqs[None, :]
    embed = jnp.concatenate([jnp.cos(angle), jnp.sin(angle)], axis=1)
    act = jnp.pad(jax.nn.silu(embed).astype(bf16), ((0, -steps_here % 16), (0, 0)))
    normed = call(
        modulate_kernel,
        jax.ShapeDtypeStruct(trajectory.shape, bf16),
        [VMEM] * 3,
        VMEM,
        [],
        MOD_COST,
    )(act, mod_weight, trajectory)

    tiles = neighbors.shape[0]
    tile = tokens // tiles
    local = neighbors - tiles * (place - 1)
    times_listed = jnp.sum(
        (local[:, :, None] == jnp.arange(3 * tiles, dtype=jnp.int32)).astype(jnp.float32), axis=1
    )
    sides = times_listed.reshape(tiles, 3, tiles)
    sides = jnp.where(place % 2 == 0, sides[:, ::-1], sides).reshape(tiles, 3 * tiles)
    mask = sides.reshape(-1)

    on_line = tok == 4 * CORES and groups == 4
    if on_line:
        inside = [(c * CORES + p, (c ^ 3) * CORES + p) for c in (1, 2) for p in range(CORES)]
        relays = [(c * CORES + p, (c ^ 1) * CORES + p) for c in (1, 2) for p in range(CORES)]
        inner = ((chip > 0) & (chip < 3)).astype(jnp.int32)
        spare = jnp.full((), tok, jnp.int32)
        last = [jnp.where(inner == 1, chip ^ 3, spare), jnp.where(inner == 1, spare, chip ^ 3)]
        chips = [chip, chip ^ 2, chip ^ 1] + last
        rows = [jnp.where(c == spare, spare, c * CORES + q) for q in (core, 1 - core) for c in chips]
        line_rows = [(chip ^ m) * CORES + q for q in (core, 1 - core) for m in (0, 2, 1, 3)]
        where = jnp.stack([group] + rows).astype(jnp.int32)
        block_rows = jnp.stack([group] + rows + line_rows).astype(jnp.int32)
        inner = inner.reshape(1)
        mine, far, near, where, block_rows, inner, mask, steps = lax.optimization_barrier(
            (
                mine,
                swap(mine, "tok", 2 * CORES),
                swap(mine, "tok", CORES),
                where,
                block_rows,
                inner,
                mask,
                steps,
            )
        )
        states = [normed] + [swap(normed, "tm", s) for s in range(1, groups)]
        places = [(s, 0) for s in range(groups)]
        middle, relayed = lax.ppermute(mine, "tok", inside), lax.ppermute(far, "tok", relays)
        kept_line = call(
            keep_kernel,
            [jax.ShapeDtypeStruct(mine.shape, bf16)] * 3,
            [HBM] * 3,
            [VMEM] * 3,
            [pltpu.SemaphoreType.DMA((3,))],
            2,
        )(mine, far, near)
        line = list(kept_line) + [middle, relayed]
        pieces = line + [swap(v, "tok", 1) for v in line]
    else:
        states = [normed] + [swap(normed, "tm", s) for s in range(1, groups)]
        places = [(s, 0) for s in range(groups)]
        pieces = [lax.all_gather(mine, "tok", axis=0, tiled=True)]
        where = block_rows = jnp.stack([group, jnp.zeros_like(group)]).astype(jnp.int32)
    depths = pieces[0].shape[0]
    held_rows = width + (depths if on_line else 0)

    def project(states, cols, normed_heads, cost):
        info = {
            "states": len(states),
            "groups": groups,
            "places": places,
            "pieces": len(pieces),
            "tokens": tokens,
            "steps": steps_here,
            "kept": kept,
            "columns": cols,
            "normed": normed_heads,
        }
        return call(
            functools.partial(project_kernel, info),
            jax.ShapeDtypeStruct((kept, tokens, cols[1]), bf16),
            [SMEM] + [VMEM] * len(states) + [HBM] * len(pieces),
            VMEM,
            [
                pltpu.VMEM((count, tokens, cols[1]), bf16),
                pltpu.VMEM((held_rows, cols[1]), bf16),
                pltpu.SemaphoreType.DMA((len(pieces),)),
            ],
            cost,
        )(where, *states, *pieces)

    if on_line:
        packed = call(
            functools.partial(pack_kernel, 3 * columns),
            jax.ShapeDtypeStruct((4 * depth, columns), bf16),
            [SMEM] + [HBM] * 5,
            VMEM,
            [pltpu.SemaphoreType.DMA((4,))],
            2,
        )(inner, *line)
        states, packed = lax.optimization_barrier((states, packed))
        beside, across = swap(packed, "tm", 1), swap(packed, "tm", 2)
        others = [beside, across, swap(halves(beside, 0)[0], "tm", 2), swap(halves(across, 0)[1], "tm", 1)]
        blocks = [[(n, 0, 3 * columns, n, depth) for n in range(10)]]
        for slot in range(2):
            blocks.append([(10 + slot + 4 * (n // 4), n % 4 * depth, 0, 10 + n, depth) for n in range(8)])
        blocks.append([(12 + n // 2 % 2 + 4 * (n // 4), n % 2 * depth, 0, 10 + n, depth) for n in range(8)])
    else:
        whole = pieces[0][:, 3 * columns :]
        out_pieces = [whole] + [swap(whole, "tm", s) for s in range(1, groups)]
        blocks = [[(slot, 0, 0, 0, width)] for slot in range(groups)]

    heads = columns // HEAD_DIM
    kv = project(states, (0, 2 * columns), heads, KV_COST)
    far_kv = lax.ppermute(kv, "tok", [(i, ((i + 1) ^ 1) - 1) for i in range(1, tok - 1)])
    near_kv = swap(kv, "tok", 1)
    states_after, _ = lax.optimization_barrier((states, kv))
    query = project(states_after, (2 * columns, columns), heads, Q_COST)
    summed = jax.ShapeDtypeStruct((steps_here, tokens, columns), bf16)
    sums = call(
        functools.partial(attention_kernel, groups, steps_here),
        [summed] * groups + ([] if spans == 1 else [jax.ShapeDtypeStruct((tokens, columns), jnp.float32)]),
        [SMEM] * 3 + [VMEM] * 4,
        [VMEM] * (groups if spans == 1 else groups + 1),
        ([pltpu.VMEM((tokens, columns), jnp.float32)] if spans == 1 else [])
        + [
            pltpu.VMEM((kept + 1, tokens, columns), bf16),
        ],
        ATT_COST,
    )(g, steps, mask, query, near_kv, kv, far_kv)
    if spans > 1:
        total = sums[groups].astype(bf16)
        members = [[s * groups + m for s in range(spans)] for m in range(groups)]
        totals = lax.all_gather(total, "tm", axis_index_groups=members).astype(jnp.float32)
        earlier = jnp.sum(
            jnp.where((jnp.arange(spans) < span)[:, None, None], totals, 0.0), axis=0
        )
        sums = [(v.astype(jnp.float32) + earlier[None]).astype(bf16) for v in sums[:groups]]
    if on_line:
        late, _ = lax.optimization_barrier((others[2:], sums))
        others = others[:2] + late
        out_pieces = pieces + others + [swap(v, "tok", 1) for v in others]
    sums = [sums[0]] + [swap(sums[s], "tm", s) for s in range(1, groups)]

    weight = call(
        functools.partial(assemble_kernel, groups, blocks),
        jax.ShapeDtypeStruct((width, width), bf16),
        [SMEM] + [HBM] * len(out_pieces),
        VMEM,
        [pltpu.VMEM((8, columns), bf16), pltpu.SemaphoreType.DMA((sum(len(each) for each in blocks),))],
        4,
    )(block_rows, *out_pieces)
    return call(
        functools.partial(out_kernel, groups),
        jax.ShapeDtypeStruct((steps_here, tokens, width), jnp.float32),
        [SMEM] + [VMEM] * (2 + groups),
        VMEM,
        [],
        4,
    )(g, start, weight, *sums)


def solution(mesh):
    return jax.shard_map(
        body,
        mesh=mesh,
        in_specs=(
            P("tok", None),
            P("tm", "tok", None),
            P(),
            P("tok", None),
            P(),
            P("tok", None),
            P("tok", None),
        ),
        out_specs=P("tm", "tok", None),
        check_vma=False,
    )
```

```python
import functools
import math

import jax
import jax.numpy as jnp
from jax import lax
from jax.experimental import pallas as pl
from jax.experimental.pallas import tpu as pltpu
from jax.sharding import PartitionSpec as P

HEADS = 12
HEAD_DIM = 128
NSCHED = 1000
CORES = 2
VMEM_LIMIT = 28 * 1024 * 1024
KV_COST, Q_COST, ATT_COST, MOD_COST = 7, 20, 6, 30
HBM = pl.BlockSpec(memory_space=pltpu.HBM)
VMEM = pl.BlockSpec(memory_space=pltpu.VMEM)
SMEM = pl.BlockSpec(memory_space=pltpu.SMEM)


def call(kernel, outs, in_specs, out_specs, scratch, cost, limit=VMEM_LIMIT):
    return pl.pallas_call(
        kernel,
        out_shape=outs,
        in_specs=in_specs,
        out_specs=out_specs,
        scratch_shapes=scratch,
        compiler_params=pltpu.CompilerParams(vmem_limit_bytes=limit),
        cost_estimate=pl.CostEstimate(flops=int(cost * 1_150_000_000), bytes_accessed=int(cost * 3_600_000), transcendentals=0),
    )


def head_groups(size):
    groups = 1
    while size % (2 * groups) == 0 and HEADS % (2 * groups) == 0:
        groups *= 2
    return groups


def swap(value, axis, mask):
    return lax.ppermute(value, axis, [(i, i ^ mask) for i in range(lax.axis_size(axis))])


def keep_kernel(*refs):
    count = len(refs) // 2
    for copy in start_all([(refs[n], refs[count + n]) for n in range(count)], refs[-1]):
        copy.wait()


def start_all(copies, sems):
    made = [pltpu.make_async_copy(src, dst, sems.at[n]) for n, (src, dst) in enumerate(copies)]
    for copy in made:
        copy.start()
    return made


def pack_kernel(at, where, *refs):
    pieces, (out, sems) = refs[:-2], refs[-2:]
    depth, columns = pieces[0].shape[0], out.shape[1]
    copies = [
        pltpu.make_async_copy(piece.at[:, pl.ds(at, columns)], out.at[pl.ds(min(n, 3) * depth, depth), :], sems.at[min(n, 3)])
        for n, piece in enumerate(pieces)
    ]
    for copy in copies[:3]:
        copy.start()

    @pl.when(where[0] == 1)
    def _():
        copies[3].start()

    @pl.when(where[0] != 1)
    def _():
        copies[4].start()

    for copy in copies[:4]:
        copy.wait()


def halves(value, axis):
    half = value.shape[axis] // 2
    return lax.slice_in_dim(value, 0, half, axis=axis), lax.slice_in_dim(value, half, None, axis=axis)


def modulate_kernel(act, weight, state, out):
    mod = jnp.dot(act[...], weight[...], preferred_element_type=jnp.float32)
    width = state.shape[-1]
    for i in range(state.shape[0]):
        values = state[i].astype(jnp.float32)
        center = values - jnp.mean(values, -1, keepdims=True)
        spread = jnp.mean(center * center, -1, keepdims=True)
        shift = mod[i : i + 1, :width]
        scale = mod[i : i + 1, width:]
        out[i] = (center / jnp.sqrt(spread + 1e-06) * (1.0 + scale) + shift).astype(jnp.bfloat16)


def head_norm(values):
    return values / jnp.sqrt(jnp.mean(values * values, -1, keepdims=True) + 1e-06)


def project_kernel(plan, where, *refs):
    states, pieces = refs[: plan["states"]], refs[plan["states"] : plan["states"] + plan["pieces"]]
    out, every, weight = refs[plan["states"] + plan["pieces"] :]
    tokens, steps_here, kept, columns = plan["tokens"], plan["steps"], plan["kept"], plan["columns"]
    depth = pieces[0].shape[0]
    for n, piece in enumerate(pieces):
        target = pl.ds(pl.multiple_of(where[1 + n] * depth, depth), depth)
        weight[target, :] = piece[:, columns[0] : columns[0] + columns[1]]

    for state, (slot, begin) in zip(states, plan["places"]):
        count, _, width = state.shape
        first = (where[0] ^ slot) * steps_here + begin
        rows = state[...].reshape(count * tokens, width)
        product = jnp.dot(rows, weight[:width, :], preferred_element_type=jnp.float32)
        for head in range(columns[1] // HEAD_DIM):
            cols = slice(head * HEAD_DIM, (head + 1) * HEAD_DIM)
            values = product[:, cols]
            if head < plan["normed"]:
                values = head_norm(values)
            values = values.astype(jnp.bfloat16).reshape(count, tokens, HEAD_DIM)
            every[pl.ds(first, count), :, cols] = values
    out[...] = every[:kept]


def attention_kernel(groups, steps_here, g_ref, steps, mask, query, near, own, far, *refs):
    outs, (total, before) = refs[:groups], refs[groups:]
    kept, tokens, columns = query.shape
    heads = columns // HEAD_DIM
    tiles = math.isqrt(mask.shape[0] // 3)
    size = tokens // tiles
    row_tile = lax.broadcasted_iota(jnp.int32, (tokens, 3 * tokens), 0) // size
    spot = row_tile * (3 * tiles) + lax.broadcasted_iota(jnp.int32, (tokens, 3 * tokens), 1) // size
    weights = jnp.zeros(spot.shape, jnp.float32)
    for n in range(mask.shape[0]):
        weights = jnp.where(spot == n, mask[n], weights)
    total[...] = jnp.zeros_like(total)
    before[0] = jnp.zeros(before.shape[1:], jnp.bfloat16)
    for k in range(kept):
        for head in range(heads):
            cols = slice(head * HEAD_DIM, (head + 1) * HEAD_DIM)
            vcols = slice(columns + head * HEAD_DIM, columns + (head + 1) * HEAD_DIM)
            keys = jnp.concatenate([near[k, :, cols], own[k, :, cols], far[k, :, cols]], axis=0)
            values = jnp.concatenate([near[k, :, vcols], own[k, :, vcols], far[k, :, vcols]], axis=0)
            score = lax.dot_general(
                query[k, :, cols],
                keys,
                (((1,), (1,)), ((), ())),
                preferred_element_type=jnp.float32,
            )
            expo = (jnp.exp2(score * (math.log2(math.e) / math.sqrt(HEAD_DIM))) * weights).astype(jnp.bfloat16)
            values = jnp.concatenate([values, jnp.ones_like(values)], axis=1)
            both = jnp.dot(expo, values, preferred_element_type=jnp.float32)
            attn = both[:, :HEAD_DIM] / both[:, HEAD_DIM:]
            total[:, cols] += steps[k] * attn.astype(jnp.bfloat16).astype(jnp.float32)
        before[k + 1] = total[...].astype(jnp.bfloat16)
    for slot, out in enumerate(outs):
        first = (g_ref[0] ^ slot) * steps_here
        for i in range(steps_here):
            out[i] = before[first + i]


def assemble_kernel(groups, blocks, where, *refs):
    pieces, (out, spare, sems) = refs[:-3], refs[-3:]
    columns = spare.shape[1]
    copies = []
    for slot in range(groups):
        cols = pl.ds(pl.multiple_of((where[0] ^ slot) * columns, columns), columns)
        for n, row, col, place, depth in blocks[slot]:
            source = pieces[n].at[pl.ds(row, depth), pl.ds(col, columns)]
            target = out.at[pl.ds(pl.multiple_of(where[1 + place] * depth, depth), depth), cols]
            copies.append((source, target, where[1 + place] * depth < out.shape[0]))
    for n, (source, target, used) in enumerate(copies):
        @pl.when(used)
        def _():
            pltpu.make_async_copy(source, target, sems.at[n]).start()
    for n, (source, target, used) in enumerate(copies):
        @pl.when(used)
        def _():
            pltpu.make_async_copy(source, target, sems.at[n]).wait()


def out_kernel(groups, where, start, weight, *refs):
    sums, (out,) = refs[:groups], refs[groups:]
    steps_here, tokens, columns = sums[0].shape
    rows = steps_here * tokens
    drift = jnp.zeros((rows, weight.shape[1]), jnp.float32)
    for slot in range(groups):
        place = pl.ds(pl.multiple_of((where[0] ^ slot) * columns, columns), columns)
        left = sums[slot][...].reshape(rows, columns)
        drift += jnp.dot(left, weight[place, :], preferred_element_type=jnp.float32)
    base = start[...].astype(jnp.float32)
    for i in range(steps_here):
        out[i] = base - drift[i * tokens : (i + 1) * tokens]


def body(start, trajectory, plan, neighbors, mod_weight, w_qkv, w_out):
    steps_here, tokens, width = trajectory.shape
    tm, tok = lax.axis_size("tm"), lax.axis_size("tok")
    groups = head_groups(tm)
    spans = tm // groups
    columns = width // groups
    depth = w_qkv.shape[0]
    index, place = lax.axis_index("tm"), lax.axis_index("tok")
    group, span = index % groups, index // groups
    chip, core = place // CORES, place % CORES
    count = groups * steps_here
    kept = count - 1 if spans == 1 else count
    bf16 = jnp.bfloat16
    g = group.astype(jnp.int32).reshape(1)

    at = group * columns
    mine = jnp.concatenate(
        [
            lax.dynamic_slice_in_dim(w_qkv, width + at, columns, axis=1),
            lax.dynamic_slice_in_dim(w_qkv, 2 * width + at, columns, axis=1),
            lax.dynamic_slice_in_dim(w_qkv, at, columns, axis=1),
            lax.dynamic_slice_in_dim(w_out, at, columns, axis=1),
        ],
        axis=1,
    )
    trajectory, mine = lax.optimization_barrier((trajectory, mine))

    times = plan.astype(jnp.float32) / NSCHED
    own_times = lax.dynamic_slice_in_dim(times, index * steps_here, steps_here)
    span_times = lax.dynamic_slice_in_dim(times, span * count, count + 1)
    steps = span_times[:-1] - span_times[1:]
    half = mod_weight.shape[0] // 2
    freqs = jnp.exp(-math.log(10000.0) * jnp.arange(half, dtype=jnp.float32) / half)
    angle = 1000.0 * own_times[:, None] * freqs[None, :]
    embed = jnp.concatenate([jnp.cos(angle), jnp.sin(angle)], axis=1)
    act = jnp.pad(jax.nn.silu(embed).astype(bf16), ((0, -steps_here % 16), (0, 0)))
    normed = call(
        modulate_kernel,
        jax.ShapeDtypeStruct(trajectory.shape, bf16),
        [VMEM] * 3,
        VMEM,
        [],
        MOD_COST,
    )(act, mod_weight, trajectory)

    tiles = neighbors.shape[0]
    tile = tokens // tiles
    local = neighbors - tiles * (place - 1)
    times_listed = jnp.sum(
        (local[:, :, None] == jnp.arange(3 * tiles, dtype=jnp.int32)).astype(jnp.float32), axis=1
    )
    sides = times_listed.reshape(tiles, 3, tiles)
    sides = jnp.where(place % 2 == 0, sides[:, ::-1], sides).reshape(tiles, 3 * tiles)
    mask = sides.reshape(-1)

    on_line = tok == 4 * CORES and groups == 4
    if on_line:
        inside = [(c * CORES + p, (c ^ 3) * CORES + p) for c in (1, 2) for p in range(CORES)]
        relays = [(c * CORES + p, (c ^ 1) * CORES + p) for c in (1, 2) for p in range(CORES)]
        inner = ((chip > 0) & (chip < 3)).astype(jnp.int32)
        spare = jnp.full((), tok, jnp.int32)
        last = [jnp.where(inner == 1, chip ^ 3, spare), jnp.where(inner == 1, spare, chip ^ 3)]
        chips = [chip, chip ^ 2, chip ^ 1] + last
        rows = [jnp.where(c == spare, spare, c * CORES + q) for q in (core, 1 - core) for c in chips]
        line_rows = [(chip ^ m) * CORES + q for q in (core, 1 - core) for m in (0, 2, 1, 3)]
        where = jnp.stack([group] + rows).astype(jnp.int32)
        block_rows = jnp.stack([group] + rows + line_rows).astype(jnp.int32)
        inner = inner.reshape(1)
        mine, far, near, where, block_rows, inner, mask, steps = lax.optimization_barrier(
            (
                mine,
                swap(mine, "tok", 2 * CORES),
                swap(mine, "tok", CORES),
                where,
                block_rows,
                inner,
                mask,
                steps,
            )
        )
        states = [normed] + [swap(normed, "tm", s) for s in range(1, groups)]
        places = [(s, 0) for s in range(groups)]
        middle, relayed = lax.ppermute(mine, "tok", inside), lax.ppermute(far, "tok", relays)
        kept_line = call(
            keep_kernel,
            [jax.ShapeDtypeStruct(mine.shape, bf16)] * 3,
            [HBM] * 3,
            [VMEM] * 3,
            [pltpu.SemaphoreType.DMA((3,))],
            2,
        )(mine, far, near)
        line = list(kept_line) + [middle, relayed]
        pieces = line + [swap(v, "tok", 1) for v in line]
    else:
        states = [normed] + [swap(normed, "tm", s) for s in range(1, groups)]
        places = [(s, 0) for s in range(groups)]
        pieces = [lax.all_gather(mine, "tok", axis=0, tiled=True)]
        where = block_rows = jnp.stack([group, jnp.zeros_like(group)]).astype(jnp.int32)
    depths = pieces[0].shape[0]
    held_rows = width + (depths if on_line else 0)

    def project(states, cols, normed_heads, cost):
        info = {
            "states": len(states),
            "groups": groups,
            "places": places,
            "pieces": len(pieces),
            "tokens": tokens,
            "steps": steps_here,
            "kept": kept,
            "columns": cols,
            "normed": normed_heads,
        }
        return call(
            functools.partial(project_kernel, info),
            jax.ShapeDtypeStruct((kept, tokens, cols[1]), bf16),
            [SMEM] + [VMEM] * (len(states) + len(pieces)),
            VMEM,
            [
                pltpu.VMEM((count, tokens, cols[1]), bf16),
                pltpu.VMEM((held_rows, cols[1]), bf16),
            ],
            cost,
        )(where, *states, *pieces)

    if on_line:
        packed = call(
            functools.partial(pack_kernel, 3 * columns),
            jax.ShapeDtypeStruct((4 * depth, columns), bf16),
            [SMEM] + [HBM] * 5,
            VMEM,
            [pltpu.SemaphoreType.DMA((4,))],
            2,
        )(inner, *line)
        states, packed = lax.optimization_barrier((states, packed))
        beside, across = swap(packed, "tm", 1), swap(packed, "tm", 2)
        others = [beside, across, swap(halves(beside, 0)[0], "tm", 2), swap(halves(across, 0)[1], "tm", 1)]
        blocks = [[(n, 0, 3 * columns, n, depth) for n in range(10)]]
        for slot in range(2):
            blocks.append([(10 + slot + 4 * (n // 4), n % 4 * depth, 0, 10 + n, depth) for n in range(8)])
        blocks.append([(12 + n // 2 % 2 + 4 * (n // 4), n % 2 * depth, 0, 10 + n, depth) for n in range(8)])
    else:
        whole = pieces[0][:, 3 * columns :]
        out_pieces = [whole] + [swap(whole, "tm", s) for s in range(1, groups)]
        blocks = [[(slot, 0, 0, 0, width)] for slot in range(groups)]

    heads = columns // HEAD_DIM
    kv = project(states, (0, 2 * columns), heads, KV_COST)
    far_kv = lax.ppermute(kv, "tok", [(i, ((i + 1) ^ 1) - 1) for i in range(1, tok - 1)])
    near_kv = swap(kv, "tok", 1)
    states_after, _ = lax.optimization_barrier((states, kv))
    query = project(states_after, (2 * columns, columns), heads, Q_COST)
    summed = jax.ShapeDtypeStruct((steps_here, tokens, columns), bf16)
    sums = call(
        functools.partial(attention_kernel, groups, steps_here),
        [summed] * groups + ([] if spans == 1 else [jax.ShapeDtypeStruct((tokens, columns), jnp.float32)]),
        [SMEM] * 3 + [VMEM] * 4,
        [VMEM] * (groups if spans == 1 else groups + 1),
        ([pltpu.VMEM((tokens, columns), jnp.float32)] if spans == 1 else [])
        + [
            pltpu.VMEM((kept + 1, tokens, columns), bf16),
        ],
        ATT_COST,
    )(g, steps, mask, query, near_kv, kv, far_kv)
    if spans > 1:
        total = sums[groups].astype(bf16)
        members = [[s * groups + m for s in range(spans)] for m in range(groups)]
        totals = lax.all_gather(total, "tm", axis_index_groups=members).astype(jnp.float32)
        earlier = jnp.sum(
            jnp.where((jnp.arange(spans) < span)[:, None, None], totals, 0.0), axis=0
        )
        sums = [(v.astype(jnp.float32) + earlier[None]).astype(bf16) for v in sums[:groups]]
    if on_line:
        late, _ = lax.optimization_barrier((others[2:], sums))
        others = others[:2] + late
        out_pieces = pieces + others + [swap(v, "tok", 1) for v in others]
    sums = [sums[0]] + [swap(sums[s], "tm", s) for s in range(1, groups)]

    weight = call(
        functools.partial(assemble_kernel, groups, blocks),
        jax.ShapeDtypeStruct((width, width), bf16),
        [SMEM] + [HBM] * len(out_pieces),
        VMEM,
        [pltpu.VMEM((8, columns), bf16), pltpu.SemaphoreType.DMA((sum(len(each) for each in blocks),))],
        4,
    )(block_rows, *out_pieces)
    return call(
        functools.partial(out_kernel, groups),
        jax.ShapeDtypeStruct((steps_here, tokens, width), jnp.float32),
        [SMEM] + [VMEM] * (2 + groups),
        VMEM,
        [],
        4,
    )(g, start, weight, *sums)


def solution(mesh):
    return jax.shard_map(
        body,
        mesh=mesh,
        in_specs=(
            P("tok", None),
            P("tm", "tok", None),
            P(),
            P("tok", None),
            P(),
            P("tok", None),
            P("tok", None),
        ),
        out_specs=P("tm", "tok", None),
        check_vma=False,
    )
```
